32 devices in a mesh: replica: 16 (over z, x, core), tensor: 2 (over y).
Axes of the slice: x: 2, y: 2, z: 4, core: 2. Of those that a mesh axis runs over, the one named last changes fastest.
Arguments:
- inputs: bfloat16 [2, 8192, 2048], P(None, 'replica', 'tensor'), may hold values from -6 to 6
- out_grads: bfloat16 [2, 8192, 2048], P(None, 'replica', 'tensor'), may hold values from -6 to 6
- gate_weight: bfloat16 [16, 2048, 2816], P('replica', None, 'tensor'), may hold values from -0.125 to 0.125
- up_weight: bfloat16 [16, 2048, 2816], P('replica', None, 'tensor'), may hold values from -0.125 to 0.125
- down_weight: bfloat16 [16, 2816, 2048], P('replica', 'tensor'), may hold values from -0.109375 to 0.109375
- rates: float32 [16], P('replica'), may hold values from 16 to 64
- partner_bits: int32 [4], replicated, may hold values from 0 to 3, each once
Outputs:
- new_gate: bfloat16 [16, 2048, 2816], P('replica', None, 'tensor')
- new_up: bfloat16 [16, 2048, 2816], P('replica', None, 'tensor')
- new_down: bfloat16 [16, 2816, 2048], P('replica', 'tensor')
- activations: bfloat16 [2, 8192, 2048], P(None, 'replica', 'tensor')
The draws below stay inside these ranges and needn't reach their ends.
Inputs may be any that keep to these rules, and one draw needn't show every extreme that they name: partner_bits holds each of the bit numbers 0, 1, 2, 3 exactly once; step s uses entry s.
All inputs are finite; a program needn't handle non-finite values.
Results may differ from the reference program's by a relative error of at most 0.024.
Values may be sent and summed in bfloat16 or wider, within the bound.
A program may use at most 192 MiB of HBM per device.

```python
import math
import jax
import jax.numpy as jnp
from jax import lax

D = 2048
FF = 2816
TOK = 512
STEPS = 2
REPLICAS = 16
TOKENS = 8192


def levels(key, dims, shards, least, high):
    factor_of, own = 1.0, jax.random.fold_in(key, 6)
    for dim, parts in shards:
        draws = jnp.exp(jax.random.uniform(jax.random.fold_in(own, dim), (parts,), jnp.float32, least / len(shards), high / len(shards)))
        factor_of = factor_of * jnp.repeat(draws, dims[dim] // parts).reshape([-1 if axis == dim else 1 for axis in range(len(dims))])
    return factor_of


def normal_values(rng, shape, width, bound, shards=(), kind=jnp.bfloat16):
    level = levels(rng, shape, shards, -0.22, 0.18) if shards else 1.0
    drawn = jax.random.normal(rng, shape, jnp.float32) * width * level
    return jnp.minimum(jnp.maximum(drawn, -bound), bound).astype(kind)


def setup_inputs(seed: int = 0) -> dict:
    keys = jax.random.split(jax.random.key(seed), 8)
    inputs = normal_values(keys[0], (STEPS, TOKENS, D), 1.0, 6.0, ((1, 16), (2, 2)))
    out_grads = normal_values(keys[1], (STEPS, TOKENS, D), 1.0, 6.0, ((1, 16), (2, 2)))
    gate_weight = normal_values(keys[2], (REPLICAS, D, FF), D ** -0.5, 0.125, ((0, 16), (2, 2)))
    up_weight = normal_values(keys[3], (REPLICAS, D, FF), D ** -0.5, 0.125, ((0, 16), (2, 2)))
    down_weight = normal_values(keys[4], (REPLICAS, FF, D), FF ** -0.5, 0.109375, ((0, 16), (1, 2)))
    rates = jnp.clip(jnp.exp(math.log(64.0) - 1.3862944 * jax.random.uniform(keys[5], (REPLICAS,), jnp.float32) ** levels(keys[5], (REPLICAS,), ((0, 16),), -0.2, 0.2)), 16.0, 64.0)
    partner_bits = jax.random.permutation(keys[6], 4).astype(jnp.int32)
    return dict(inputs=inputs, out_grads=out_grads, gate_weight=gate_weight, up_weight=up_weight, down_weight=down_weight, rates=rates, partner_bits=partner_bits)


def local_pass(weights, inputs, grads_out):
    gate_w, up_w, down_w = weights
    gate = jnp.dot(inputs, gate_w, preferred_element_type=jnp.float32)
    up = jnp.dot(inputs, up_w, preferred_element_type=jnp.float32)
    sigma = jax.nn.sigmoid(gate)
    active = gate * sigma
    hidden = (active * up).astype(jnp.bfloat16)
    mixed = jnp.dot(hidden, down_w, preferred_element_type=jnp.float32)
    back = lax.dot_general(grads_out, down_w, (((1,), (1,)), ((), ())), preferred_element_type=jnp.float32)
    d_gate = (back * up * sigma * (1.0 + gate * (1.0 - sigma))).astype(jnp.bfloat16)
    d_up = (back * active).astype(jnp.bfloat16)
    grad_down = lax.dot_general(hidden, grads_out, (((0,), (0,)), ((), ())), preferred_element_type=jnp.float32)
    grad_gate = lax.dot_general(inputs, d_gate, (((0,), (0,)), ((), ())), preferred_element_type=jnp.float32)
    grad_up = lax.dot_general(inputs, d_up, (((0,), (0,)), ((), ())), preferred_element_type=jnp.float32)
    return (mixed, (grad_gate, grad_up, grad_down))

def squares_of(grads):
    return sum((jnp.sum(g * g) for g in grads))

def apply_update(weights, grads, squares, rate):
    scale = rate / jnp.sqrt(squares + 1e-06)
    return tuple(((w.astype(jnp.float32) - scale * g).astype(jnp.bfloat16) for w, g in zip(weights, grads)))

def average(first, second):
    return tuple((((a.astype(jnp.float32) + b.astype(jnp.float32)) * 0.5).astype(jnp.bfloat16) for a, b in zip(first, second)))

def reference(inputs, out_grads, gate_weight, up_weight, down_weight, rates, partner_bits):
    replica_ids = jnp.arange(REPLICAS, dtype=jnp.int32)
    weights = (gate_weight, up_weight, down_weight)
    results = []
    for step in range(STEPS):
        tokens = inputs[step].reshape(REPLICAS, TOK, D)
        grads_out = out_grads[step].reshape(REPLICAS, TOK, D)

        def one_replica(packed):
            gate_w, up_w, down_w, tok_rows, grad_rows, rate = packed
            mixed, grads = local_pass((gate_w, up_w, down_w), tok_rows, grad_rows)
            fresh = apply_update((gate_w, up_w, down_w), grads, squares_of(grads), rate)
            return (mixed.astype(jnp.bfloat16), fresh)
        mixed, fresh = lax.map(one_replica, (weights[0], weights[1], weights[2], tokens, grads_out, rates))
        partner = jnp.bitwise_xor(replica_ids, jnp.left_shift(jnp.int32(1), partner_bits[step].astype(jnp.int32)))
        other = tuple((jnp.take(f, partner, axis=0) for f in fresh))
        weights = average(fresh, other)
        results.append(mixed.reshape(TOKENS, D))
    return (weights[0], weights[1], weights[2], jnp.stack(results))
```

```python
from functools import partial

import jax
import jax.numpy as jnp
from jax import lax
from jax.experimental import pallas as pl
from jax.experimental.pallas import tpu as pltpu
from jax.sharding import PartitionSpec as P

DEPTH = 3
COST = (0.17, 1.0, 1.0, 2.0)


def dot_t(a, b):
    return lax.dot_general(a, b, (((0,), (0,)), ((), ())), preferred_element_type=jnp.float32)


def dot_r(a, b):
    return lax.dot_general(a, b, (((1,), (1,)), ((), ())), preferred_element_type=jnp.float32)


def forward(weights, x, dy):
    gate_w, up_w, down_w = weights
    gate = jnp.dot(x, gate_w, preferred_element_type=jnp.float32)
    up = jnp.dot(x, up_w, preferred_element_type=jnp.float32)
    sigma = jax.nn.sigmoid(gate)
    active = gate * sigma
    hidden = (active * up).astype(jnp.bfloat16)
    back = dot_r(dy, down_w)
    d_gate = (back * up * sigma * (1.0 + gate * (1.0 - sigma))).astype(jnp.bfloat16)
    d_up = (back * active).astype(jnp.bfloat16)
    return hidden, d_gate, d_up


def squares_of(x, dy, hidden, d_gate, d_up):
    gates = dot_r(d_gate, d_gate) + dot_r(d_up, d_up)
    return jnp.sum(dot_r(x, x) * gates) + jnp.sum(dot_r(dy, dy) * dot_r(hidden, hidden))


def scale_of(rate, squares):
    return rate / jnp.sqrt(jnp.maximum(squares, 0.0) + 1e-06)


def fresh(weight, left, right, scale):
    return (weight.astype(jnp.float32) - scale * dot_t(left, right)).astype(jnp.bfloat16)


def mean(a, b):
    return ((a.astype(jnp.float32) + b.astype(jnp.float32)) * 0.5).astype(jnp.bfloat16)


def output(hidden, down_w):
    mixed = jnp.dot(hidden, down_w, preferred_element_type=jnp.float32)
    return lax.psum_scatter(
        mixed.astype(jnp.bfloat16), "tensor", scatter_dimension=1, tiled=True
    )


def gather(value):
    return lax.all_gather(value, "tensor", axis=value.ndim - 1, tiled=True)


def parts_of(rows):
    return max(p for p in (2, 4) if rows % (16 * p) == 0)


def kernel(first, second, ranks, *refs):
    fresh_refs, tokens, refs = refs[:3], refs[3], refs[4:]
    own_refs, far_refs, theirs, refs = refs[:3], refs[3:6], refs[6], refs[7:]
    held, landed, sems = refs[:3], refs[3:6], refs[6:]
    load, store, send1, recv1, send2, recv2, send3, recv3, token_send, token_recv = sems
    me, t = lax.axis_index("replica"), lax.axis_index("tensor")

    def partner(bit):
        side = (me // 2**bit) % 2
        return me + (1 - 2 * side) * 2**bit

    near, far = {"replica": partner(first)}, {"replica": partner(second)}
    peers = [{"tensor": lax.rem(t + k, ranks)} for k in range(1, ranks)]
    role = (me // 2**first) % 2
    shared = COST[first] < COST[second]

    chunks = []
    for m in range(3):
        parts = parts_of(held[m].shape[0])
        size = held[m].shape[0] // parts
        chunks += [(m, i, size) for i in range(parts)]
    count = len(chunks)

    def copy_of(src, dst, send, recv, to):
        return pltpu.make_async_remote_copy(
            src_ref=src, dst_ref=dst, send_sem=send, recv_sem=recv, device_id=to,
            device_id_type=pl.DeviceIdType.MESH,
        )

    def rows(c):
        m, i, size = chunks[c]
        return m, pl.ds(i * size, size)

    def loading(c):
        m, at = rows(c)
        return pltpu.make_async_copy(fresh_refs[m].at[at], held[m].at[at], load.at[c])

    def storing(c):
        m, at = rows(c)
        return pltpu.make_async_copy(landed[m].at[at], own_refs[m].at[at], store.at[c])

    def swapping(c):
        m, at = rows(c)
        return copy_of(fresh_refs[m].at[at], landed[m].at[at], send1.at[c], recv1.at[c], near)

    def fetching(c):
        m, at = rows(c)
        return copy_of(landed[m].at[at], far_refs[m].at[at], send2.at[c], recv2.at[c], far)

    def half(pair, which):
        m, i, size = chunks[2 * pair]
        return m, pl.ds(pl.multiple_of((i + which) * size, 16), size)

    def fetching_half(pair):
        m, at = half(pair, role)
        return copy_of(landed[m].at[at], far_refs[m].at[at], send2.at[pair], recv2.at[pair], far)

    def passing(pair):
        m, at = half(pair, role)
        return copy_of(far_refs[m].at[at], far_refs[m].at[at], send3.at[pair], recv3.at[pair], near)

    width = tokens.shape[-1]
    columns = theirs.at[:, :, pl.ds(pl.multiple_of(t * width, width), width)]
    tokens_out = copy_of(tokens, columns, token_send.at[0], token_recv.at[0], far)
    spread = [
        copy_of(columns, columns, token_send.at[k + 1], token_recv.at[k + 1], peers[k])
        for k in range(ranks - 1)
    ]

    barrier = pltpu.get_barrier_semaphore()
    for to in [near, far] + peers:
        pl.semaphore_signal(barrier, inc=1, device_id=to, device_id_type=pl.DeviceIdType.MESH)
    pl.semaphore_wait(barrier, 1 + ranks)

    tokens_out.start()
    for c in range(DEPTH):
        swapping(c).start()
    for c in range(count):
        loading(c).start()
    token_step = count - 1 if COST[first] < 1 else count // 2
    passed = 0

    def pass_on(pair):
        fetching_half(pair).wait_recv()
        passing(pair).start()

    for c in range(count):
        m, i, size = chunks[c]
        loading(c).wait()
        swapping(c).wait()
        if c + DEPTH < count:
            swapping(c + DEPTH).start()
        step = 32 if size % 32 == 0 else 16

        def average(k, carry, m=m, i=i, size=size, step=step):
            at = pl.ds(pl.multiple_of(i * size + k * step, step), step)
            mine = held[m][at].astype(jnp.float32)
            other = landed[m][at].astype(jnp.float32)
            landed[m][at] = ((mine + other) * 0.5).astype(jnp.bfloat16)
            return carry

        lax.fori_loop(0, size // step, average, 0)
        storing(c).start()
        if not shared:
            fetching(c).start()
        elif c % 2 == 1:
            fetching_half(c // 2).start()
            if c >= 5:
                pass_on(passed)
                passed += 1
        if c == token_step:
            tokens_out.wait_recv()
            for copy in spread:
                copy.start()
    if shared:
        for pair in range(passed, count // 2):
            pass_on(pair)
        for pair in range(count // 2):
            fetching_half(pair).wait_send()
            passing(pair).wait()
    else:
        for c in range(count):
            fetching(c).wait()
    for c in range(count):
        storing(c).wait()
    tokens_out.wait_send()
    for copy in spread:
        copy.wait()


def stream(first, second, number, operands):
    weights, tokens = operands
    ranks = lax.axis_size("tensor")
    count = sum(parts_of(w.shape[0]) for w in weights)
    like = [jax.ShapeDtypeStruct(w.shape, w.dtype) for w in weights]
    theirs = jax.ShapeDtypeStruct(
        tokens.shape[:-1] + (tokens.shape[-1] * ranks,), tokens.dtype
    )
    whole = pl.BlockSpec(memory_space=pl.ANY)
    held = [pltpu.VMEM(w.shape, w.dtype) for w in weights]
    size = sum(w.size * 2 for w in weights)
    result = pl.pallas_call(
        partial(kernel, first, second, ranks),
        out_shape=like + like + [theirs],
        in_specs=[whole] * 4,
        out_specs=[whole] * 7,
        scratch_shapes=held
        + held
        + [pltpu.SemaphoreType.DMA((count,))] * 8
        + [pltpu.SemaphoreType.DMA((ranks,))] * 2,
        compiler_params=pltpu.CompilerParams(
            collective_id=number, has_side_effects=True, vmem_limit_bytes=48 * 2**20
        ),
        cost_estimate=pl.CostEstimate(flops=size, bytes_accessed=4 * size, transcendentals=0),
        name=f"stream_{first}_{second}",
    )(*weights, tokens)
    return tuple(result[:3]), tuple(result[3:6]), result[6]


def local(inputs, out_grads, gate_weight, up_weight, down_weight, rates, partner_bits):
    weights = (gate_weight[0], up_weight[0], down_weight[0])
    rate = rates[0]
    x, dy = gather(inputs[0]), gather(out_grads[0])
    tokens = jnp.stack([inputs[1], out_grads[1]])
    mine = gather(tokens)

    hidden, d_gate, d_up = forward(weights, x, dy)
    scale = scale_of(rate, lax.psum(squares_of(x, dy, hidden, d_gate, d_up), "tensor"))
    results = [output(hidden, weights[2])]
    updated = tuple(
        fresh(weight, left, right, scale)
        for weight, left, right in zip(weights, (x, x, hidden), (d_gate, d_up, dy))
    )

    bits = len(COST)
    plans = [(a, b) for a in range(bits) for b in range(bits) if a != b]
    first, second = partner_bits[0], partner_bits[1]
    index = first * (bits - 1) + second - (second > first).astype(second.dtype)
    all_rates = lax.all_gather(rates, "replica", tiled=True)
    far_rate = all_rates[lax.axis_index("replica") ^ (1 << second)]
    own, far, theirs = lax.switch(
        index,
        [partial(stream, a, b, number) for number, (a, b) in enumerate(plans)],
        (updated, tokens),
    )

    hidden, d_gate, d_up = forward(own, mine[0], mine[1])
    far_hidden, far_gate, far_up = forward(far, theirs[0], theirs[1])
    squares = lax.psum(
        jnp.stack(
            [
                squares_of(mine[0], mine[1], hidden, d_gate, d_up),
                squares_of(theirs[0], theirs[1], far_hidden, far_gate, far_up),
            ]
        ),
        "tensor",
    )
    results.append(output(hidden, own[2]))
    scale, far_scale = scale_of(rate, squares[0]), scale_of(far_rate, squares[1])
    done = []
    for a, b, l, r, fl, fr in zip(
        own,
        far,
        (mine[0], mine[0], hidden),
        (d_gate, d_up, mine[1]),
        (theirs[0], theirs[0], far_hidden),
        (far_gate, far_up, theirs[1]),
    ):
        done.append(mean(fresh(a, l, r, scale), fresh(b, fl, fr, far_scale))[None])
    return (done[0], done[1], done[2], jnp.stack(results))


def solution(mesh):
    return jax.shard_map(
        local,
        mesh=mesh,
        in_specs=(
            P(None, "replica", "tensor"),
            P(None, "replica", "tensor"),
            P("replica", None, "tensor"),
            P("replica", None, "tensor"),
            P("replica", "tensor", None),
            P("replica"),
            P(),
        ),
        out_specs=(
            P("replica", None, "tensor"),
            P("replica", None, "tensor"),
            P("replica", "tensor", None),
            P(None, "replica", "tensor"),
        ),
        check_vma=False,
    )
```

```python
from functools import partial

import jax
import jax.numpy as jnp
from jax import lax
from jax.experimental import pallas as pl
from jax.experimental.pallas import tpu as pltpu
from jax.sharding import PartitionSpec as P

DEPTH = 3
COST = (0.17, 1.0, 1.0, 2.0)


def dot_t(a, b):
    return lax.dot_general(a, b, (((0,), (0,)), ((), ())), preferred_element_type=jnp.float32)


def dot_r(a, b):
    return lax.dot_general(a, b, (((1,), (1,)), ((), ())), preferred_element_type=jnp.float32)


def forward(weights, x, dy):
    gate_w, up_w, down_w = weights
    gate = jnp.dot(x, gate_w, preferred_element_type=jnp.float32)
    up = jnp.dot(x, up_w, preferred_element_type=jnp.float32)
    sigma = jax.nn.sigmoid(gate)
    active = gate * sigma
    hidden = (active * up).astype(jnp.bfloat16)
    back = dot_r(dy, down_w)
    d_gate = (back * up * sigma * (1.0 + gate * (1.0 - sigma))).astype(jnp.bfloat16)
    d_up = (back * active).astype(jnp.bfloat16)
    return lax.optimization_barrier((hidden, d_gate, d_up))


def squares_of(x, dy, hidden, d_gate, d_up):
    gates = dot_r(d_gate, d_gate) + dot_r(d_up, d_up)
    return jnp.sum(dot_r(x, x) * gates) + jnp.sum(dot_r(dy, dy) * dot_r(hidden, hidden))


def scale_of(rate, squares):
    return rate / jnp.sqrt(jnp.maximum(squares, 0.0) + 1e-06)


def update_kernel(turned, scale, *refs):
    out = refs[-1]
    values = []
    for k in range(len(refs) // 3):
        weight, left, right = refs[3 * k : 3 * k + 3]
        dims = (((1,), (0,)), ((), ())) if turned else (((0,), (0,)), ((), ()))
        grad = lax.dot_general(
            left[...], right[...], dims, preferred_element_type=jnp.float32
        )
        value = weight[...].astype(jnp.float32) - scale[k] * grad
        values.append(value.astype(jnp.bfloat16))
    if len(values) == 1:
        out[...] = values[0]
    else:
        total = values[0].astype(jnp.float32) + values[1].astype(jnp.float32)
        out[...] = (total * 0.5).astype(jnp.bfloat16)


def update(turned, scale, *triples):
    weight = triples[0][0]
    height, columns = weight.shape
    tall = triples[0][2].shape[0]
    size = height // (8 if height % 128 == 0 else 2)
    block = pl.BlockSpec((size, columns), lambda i: (i, 0))
    if turned:
        left = pl.BlockSpec((size, tall), lambda i: (i, 0))
    else:
        left = pl.BlockSpec((tall, size), lambda i: (0, i))
    right = pl.BlockSpec((tall, columns), lambda i: (0, 0))
    count = len(triples)
    return pl.pallas_call(
        partial(update_kernel, turned),
        grid=(height // size,),
        out_shape=jax.ShapeDtypeStruct(weight.shape, weight.dtype),
        in_specs=[pl.BlockSpec(memory_space=pltpu.SMEM)] + [block, left, right] * count,
        out_specs=block,
        compiler_params=pltpu.CompilerParams(vmem_limit_bytes=40 * 2**20),
        cost_estimate=pl.CostEstimate(
            flops=2 * count * height * columns * tall,
            bytes_accessed=2 * (count + 1) * height * columns,
            transcendentals=0,
        ),
        name=f"update_{count}",
    )(scale, *[part for triple in triples for part in triple])


def output(hidden, down_w):
    mixed = jnp.dot(hidden, down_w, preferred_element_type=jnp.float32)
    return lax.psum_scatter(
        mixed.astype(jnp.bfloat16), "tensor", scatter_dimension=1, tiled=True
    )


def gather(value):
    return lax.all_gather(value, "tensor", axis=value.ndim - 1, tiled=True)


def parts_of(rows):
    return max(p for p in (2, 4) if rows % (16 * p) == 0)


def kernel(first, second, ranks, *refs):
    fresh_refs, tokens, rate, refs = refs[:3], refs[3], refs[4], refs[5:]
    own_refs, far_refs, theirs, ours, far_rate = refs[:3], refs[3:6], refs[6], refs[7], refs[8]
    refs = refs[9:]
    held, landed, sems = refs[:3], refs[3:6], refs[6:]
    load, store, send1, recv1, send2, recv2, send3, recv3, token_send, token_recv = sems
    me, t = lax.axis_index("replica"), lax.axis_index("tensor")

    def partner(bit):
        side = (me // 2**bit) % 2
        return me + (1 - 2 * side) * 2**bit

    near, far = {"replica": partner(first)}, {"replica": partner(second)}
    peers = [{"tensor": lax.rem(t + k, ranks)} for k in range(1, ranks)]
    role = (me // 2**first) % 2
    shared = COST[first] < COST[second]

    chunks = []
    for m in range(3):
        parts = parts_of(held[m].shape[0])
        size = held[m].shape[0] // parts
        chunks += [(m, i, size) for i in range(parts)]
    count = len(chunks)

    def copy_of(src, dst, send, recv, to):
        return pltpu.make_async_remote_copy(
            src_ref=src, dst_ref=dst, send_sem=send, recv_sem=recv, device_id=to,
            device_id_type=pl.DeviceIdType.MESH,
        )

    def rows(c):
        m, i, size = chunks[c]
        return m, pl.ds(i * size, size)

    def loading(c):
        m, at = rows(c)
        return pltpu.make_async_copy(fresh_refs[m].at[at], held[m].at[at], load.at[c])

    def storing(c):
        m, at = rows(c)
        return pltpu.make_async_copy(landed[m].at[at], own_refs[m].at[at], store.at[c])

    def swapping(c):
        m, at = rows(c)
        return copy_of(fresh_refs[m].at[at], landed[m].at[at], send1.at[c], recv1.at[c], near)

    def fetching(c):
        m, at = rows(c)
        return copy_of(landed[m].at[at], far_refs[m].at[at], send2.at[c], recv2.at[c], far)

    def half(pair, which):
        m, i, size = chunks[2 * pair]
        return m, pl.ds(pl.multiple_of((i + which) * size, 16), size)

    def fetching_half(pair):
        m, at = half(pair, role)
        return copy_of(landed[m].at[at], far_refs[m].at[at], send2.at[pair], recv2.at[pair], far)

    def passing(pair):
        m, at = half(pair, role)
        return copy_of(far_refs[m].at[at], far_refs[m].at[at], send3.at[pair], recv3.at[pair], near)

    width = tokens.shape[-1]
    columns = theirs.at[:, :, pl.ds(pl.multiple_of(t * width, width), width)]
    tokens_out = copy_of(tokens, columns, token_send.at[0], token_recv.at[0], far)
    spread = [
        copy_of(columns, columns, token_send.at[k + 1], token_recv.at[k + 1], peers[k])
        for k in range(ranks - 1)
    ]
    place = ours.at[:, :, pl.ds(pl.multiple_of(t * width, width), width)]
    early = [
        copy_of(tokens, place, token_send.at[ranks + k], token_recv.at[ranks + k], peers[k])
        for k in range(ranks - 1)
    ]
    early.append(pltpu.make_async_copy(tokens, place, token_send.at[2 * ranks - 1]))
    early.append(
        copy_of(rate, far_rate, token_send.at[2 * ranks], token_recv.at[2 * ranks], far)
    )

    barrier = pltpu.get_barrier_semaphore()
    for to in [near, far] + peers:
        pl.semaphore_signal(barrier, inc=1, device_id=to, device_id_type=pl.DeviceIdType.MESH)
    pl.semaphore_wait(barrier, 1 + ranks)

    tokens_out.start()
    for c in range(DEPTH):
        swapping(c).start()
    for copy in early:
        copy.start()
    for c in range(count):
        loading(c).start()
    token_step = count - 1 if COST[first] < 1 else count // 2
    passed = 0

    def pass_on(pair):
        fetching_half(pair).wait_recv()
        passing(pair).start()

    for c in range(count):
        m, i, size = chunks[c]
        loading(c).wait()
        swapping(c).wait()
        if c + DEPTH < count:
            swapping(c + DEPTH).start()
        step = 32 if size % 32 == 0 else 16

        def average(k, carry, m=m, i=i, size=size, step=step):
            at = pl.ds(pl.multiple_of(i * size + k * step, step), step)
            mine = held[m][at].astype(jnp.float32)
            other = landed[m][at].astype(jnp.float32)
            landed[m][at] = ((mine + other) * 0.5).astype(jnp.bfloat16)
            return carry

        lax.fori_loop(0, size // step, average, 0)
        storing(c).start()
        if not shared:
            fetching(c).start()
        elif c % 2 == 1:
            fetching_half(c // 2).start()
            if c >= 5:
                pass_on(passed)
                passed += 1
        if c == token_step:
            tokens_out.wait_recv()
            for copy in spread:
                copy.start()
    if shared:
        for pair in range(passed, count // 2):
            pass_on(pair)
        for pair in range(count // 2):
            fetching_half(pair).wait_send()
            passing(pair).wait()
    else:
        for c in range(count):
            fetching(c).wait()
    for c in range(count):
        storing(c).wait()
    tokens_out.wait_send()
    for copy in spread + early:
        copy.wait()


def stream(first, second, number, operands):
    weights, tokens, rate = operands
    ranks = lax.axis_size("tensor")
    count = sum(parts_of(w.shape[0]) for w in weights)
    like = [jax.ShapeDtypeStruct(w.shape, w.dtype) for w in weights]
    theirs = jax.ShapeDtypeStruct(
        tokens.shape[:-1] + (tokens.shape[-1] * ranks,), tokens.dtype
    )
    whole = pl.BlockSpec(memory_space=pl.ANY)
    held = [pltpu.VMEM(w.shape, w.dtype) for w in weights]
    size = sum(w.size * 2 for w in weights)
    result = pl.pallas_call(
        partial(kernel, first, second, ranks),
        out_shape=like + like + [theirs, theirs, jax.ShapeDtypeStruct(rate.shape, rate.dtype)],
        in_specs=[whole] * 5,
        out_specs=[whole] * 9,
        scratch_shapes=held
        + held
        + [pltpu.SemaphoreType.DMA((count,))] * 8
        + [pltpu.SemaphoreType.DMA((2 * ranks + 1,))] * 2,
        compiler_params=pltpu.CompilerParams(
            collective_id=number, has_side_effects=True, vmem_limit_bytes=48 * 2**20
        ),
        cost_estimate=pl.CostEstimate(flops=size, bytes_accessed=4 * size, transcendentals=0),
        name=f"stream_{first}_{second}",
    )(*weights, tokens, rate)
    return tuple(result[:3]), tuple(result[3:6]), result[6], result[7], result[8]


def local(inputs, out_grads, gate_weight, up_weight, down_weight, rates, partner_bits):
    weights = (gate_weight[0], up_weight[0], down_weight[0])
    rate = rates[0]
    x, dy = gather(inputs[0]), gather(out_grads[0])
    tokens = jnp.stack([inputs[1], out_grads[1]])

    hidden, d_gate, d_up = forward(weights, x, dy)
    scale = scale_of(rate, lax.psum(squares_of(x, dy, hidden, d_gate, d_up), "tensor"))
    results = [output(hidden, weights[2])]
    scale = scale[None]
    updated = (
        update(False, scale, (weights[0], x, d_gate)),
        update(False, scale, (weights[1], x, d_up)),
        update(True, scale, (weights[2], hidden.T, dy)),
    )

    bits = len(COST)
    plans = [(a, b) for a in range(bits) for b in range(bits) if a != b]
    first, second = partner_bits[0], partner_bits[1]
    index = first * (bits - 1) + second - (second > first).astype(second.dtype)
    own, far, theirs, mine, far_rate = lax.switch(
        index,
        [partial(stream, a, b, number) for number, (a, b) in enumerate(plans)],
        (updated, tokens, jnp.full((8, 128), rate)),
    )

    hidden, d_gate, d_up = forward(own, mine[0], mine[1])
    far_hidden, far_gate, far_up = forward(far, theirs[0], theirs[1])
    squares = lax.psum(
        jnp.stack(
            [
                squares_of(mine[0], mine[1], hidden, d_gate, d_up),
                squares_of(theirs[0], theirs[1], far_hidden, far_gate, far_up),
            ]
        ),
        "tensor",
    )
    results.append(output(hidden, own[2]))
    scale = jnp.stack([scale_of(rate, squares[0]), scale_of(far_rate[0, 0], squares[1])])
    done = (
        update(False, scale, (own[0], mine[0], d_gate), (far[0], theirs[0], far_gate)),
        update(False, scale, (own[1], mine[0], d_up), (far[1], theirs[0], far_up)),
        update(True, scale, (own[2], hidden.T, mine[1]), (far[2], far_hidden.T, theirs[1])),
    )
    return (done[0][None], done[1][None], done[2][None], jnp.stack(results))


def solution(mesh):
    return jax.shard_map(
        local,
        mesh=mesh,
        in_specs=(
            P(None, "replica", "tensor"),
            P(None, "replica", "tensor"),
            P("replica", None, "tensor"),
            P("replica", None, "tensor"),
            P("replica", "tensor", None),
            P("replica"),
            P(),
        ),
        out_specs=(
            P("replica", None, "tensor"),
            P("replica", None, "tensor"),
            P("replica", "tensor", None),
            P(None, "replica", "tensor"),
        ),
        check_vma=False,
    )
```

```python
from functools import partial

import jax
import jax.numpy as jnp
from jax import lax
from jax.experimental import pallas as pl
from jax.experimental.pallas import tpu as pltpu
from jax.sharding import PartitionSpec as P

DEPTH = 3
COST = (0.17, 1.0, 1.0, 2.0)


def dot_t(a, b):
    return lax.dot_general(a, b, (((0,), (0,)), ((), ())), preferred_element_type=jnp.float32)


def dot_r(a, b):
    return lax.dot_general(a, b, (((1,), (1,)), ((), ())), preferred_element_type=jnp.float32)


def forward(weights, x, dy):
    gate_w, up_w, down_w = weights
    gate = jnp.dot(x, gate_w, preferred_element_type=jnp.float32)
    up = jnp.dot(x, up_w, preferred_element_type=jnp.float32)
    sigma = jax.nn.sigmoid(gate)
    active = gate * sigma
    hidden = (active * up).astype(jnp.bfloat16)
    back = dot_r(dy, down_w)
    d_gate = (back * up * sigma * (1.0 + gate * (1.0 - sigma))).astype(jnp.bfloat16)
    d_up = (back * active).astype(jnp.bfloat16)
    return lax.optimization_barrier((hidden, d_gate, d_up))


def squares_of(x, dy, hidden, d_gate, d_up):
    gates = dot_r(d_gate, d_gate) + dot_r(d_up, d_up)
    return jnp.sum(dot_r(x, x) * gates) + jnp.sum(dot_r(dy, dy) * dot_r(hidden, hidden))


def scale_of(rate, squares):
    return rate / jnp.sqrt(jnp.maximum(squares, 0.0) + 1e-06)


def update_kernel(turned, scale, *refs):
    out = refs[-1]
    values = []
    for k in range(len(refs) // 3):
        weight, left, right = refs[3 * k : 3 * k + 3]
        dims = (((1,), (0,)), ((), ())) if turned else (((0,), (0,)), ((), ()))
        grad = lax.dot_general(
            left[...], right[...], dims, preferred_element_type=jnp.float32
        )
        value = weight[...].astype(jnp.float32) - scale[k] * grad
        values.append(value.astype(jnp.bfloat16))
    if len(values) == 1:
        out[...] = values[0]
    else:
        total = values[0].astype(jnp.float32) + values[1].astype(jnp.float32)
        out[...] = (total * 0.5).astype(jnp.bfloat16)


def update(turned, scale, *triples):
    weight = triples[0][0]
    height, columns = weight.shape
    tall = triples[0][2].shape[0]
    size = height // (8 if height % 128 == 0 else 2)
    block = pl.BlockSpec((size, columns), lambda i: (i, 0))
    if turned:
        left = pl.BlockSpec((size, tall), lambda i: (i, 0))
    else:
        left = pl.BlockSpec((tall, size), lambda i: (0, i))
    right = pl.BlockSpec((tall, columns), lambda i: (0, 0))
    count = len(triples)
    return pl.pallas_call(
        partial(update_kernel, turned),
        grid=(height // size,),
        out_shape=jax.ShapeDtypeStruct(weight.shape, weight.dtype),
        in_specs=[pl.BlockSpec(memory_space=pltpu.SMEM)] + [block, left, right] * count,
        out_specs=block,
        compiler_params=pltpu.CompilerParams(vmem_limit_bytes=40 * 2**20),
        cost_estimate=pl.CostEstimate(
            flops=2 * count * height * columns * tall,
            bytes_accessed=2 * (count + 1) * height * columns,
            transcendentals=0,
        ),
        name=f"update_{count}",
    )(scale, *[part for triple in triples for part in triple])


def output(hidden, down_w):
    mixed = jnp.dot(hidden, down_w, preferred_element_type=jnp.float32)
    return lax.psum_scatter(
        mixed.astype(jnp.bfloat16), "tensor", scatter_dimension=1, tiled=True
    )


def gather(value):
    if lax.axis_size("tensor") != 2:
        return lax.all_gather(value, "tensor", axis=value.ndim - 1, tiled=True)
    other = lax.ppermute(value, "tensor", [(0, 1), (1, 0)])
    is_first = lax.axis_index("tensor") == 0
    left, right = jnp.where(is_first, value, other), jnp.where(is_first, other, value)
    return jnp.concatenate([left, right], axis=-1)


def parts_of(rows):
    return max(p for p in (2, 4) if rows % (16 * p) == 0)


def kernel(first, second, ranks, *refs):
    fresh_refs, tokens, rate, refs = refs[:3], refs[3], refs[4], refs[5:]
    own_refs, far_refs, theirs, ours, far_rate = refs[:3], refs[3:6], refs[6], refs[7], refs[8]
    refs = refs[9:]
    held, landed, sems = refs[:3], refs[3:6], refs[6:]
    load, store, send1, recv1, send2, recv2, send3, recv3, token_send, token_recv = sems
    me, t = lax.axis_index("replica"), lax.axis_index("tensor")

    def partner(bit):
        side = (me // 2**bit) % 2
        return me + (1 - 2 * side) * 2**bit

    near, far = {"replica": partner(first)}, {"replica": partner(second)}
    peers = [{"tensor": lax.rem(t + k, ranks)} for k in range(1, ranks)]
    role = (me // 2**first) % 2
    shared = COST[first] < COST[second]

    chunks = []
    for m in range(3):
        parts = parts_of(held[m].shape[0])
        size = held[m].shape[0] // parts
        chunks += [(m, i, size) for i in range(parts)]
    count = len(chunks)

    def copy_of(src, dst, send, recv, to):
        return pltpu.make_async_remote_copy(
            src_ref=src, dst_ref=dst, send_sem=send, recv_sem=recv, device_id=to,
            device_id_type=pl.DeviceIdType.MESH,
        )

    def rows(c):
        m, i, size = chunks[c]
        return m, pl.ds(i * size, size)

    def loading(c):
        m, at = rows(c)
        return pltpu.make_async_copy(fresh_refs[m].at[at], held[m].at[at], load.at[c])

    def storing(c):
        m, at = rows(c)
        return pltpu.make_async_copy(landed[m].at[at], own_refs[m].at[at], store.at[c])

    def swapping(c):
        m, at = rows(c)
        return copy_of(fresh_refs[m].at[at], landed[m].at[at], send1.at[c], recv1.at[c], near)

    def fetching(c):
        m, at = rows(c)
        return copy_of(landed[m].at[at], far_refs[m].at[at], send2.at[c], recv2.at[c], far)

    def half(pair, which):
        m, i, size = chunks[2 * pair]
        return m, pl.ds(pl.multiple_of((i + which) * size, 16), size)

    def fetching_half(pair):
        m, at = half(pair, role)
        return copy_of(landed[m].at[at], far_refs[m].at[at], send2.at[pair], recv2.at[pair], far)

    def passing(pair):
        m, at = half(pair, role)
        return copy_of(far_refs[m].at[at], far_refs[m].at[at], send3.at[pair], recv3.at[pair], near)

    width = tokens.shape[-1]
    columns = theirs.at[:, :, pl.ds(pl.multiple_of(t * width, width), width)]
    tokens_out = copy_of(tokens, columns, token_send.at[0], token_recv.at[0], far)
    spread = [
        copy_of(columns, columns, token_send.at[k + 1], token_recv.at[k + 1], peers[k])
        for k in range(ranks - 1)
    ]
    place = ours.at[:, :, pl.ds(pl.multiple_of(t * width, width), width)]
    early = [
        copy_of(tokens, place, token_send.at[ranks + k], token_recv.at[ranks + k], peers[k])
        for k in range(ranks - 1)
    ]
    early.append(pltpu.make_async_copy(tokens, place, token_send.at[2 * ranks - 1]))
    early.append(
        copy_of(rate, far_rate, token_send.at[2 * ranks], token_recv.at[2 * ranks], far)
    )

    barrier = pltpu.get_barrier_semaphore()
    for to in [near, far] + peers:
        pl.semaphore_signal(barrier, inc=1, device_id=to, device_id_type=pl.DeviceIdType.MESH)
    pl.semaphore_wait(barrier, 1 + ranks)

    tokens_out.start()
    for c in range(DEPTH):
        swapping(c).start()
    for copy in early:
        copy.start()
    for c in range(count):
        loading(c).start()
    token_step = count - 1 if COST[first] < 1 else count // 2
    passed = 0

    def pass_on(pair):
        fetching_half(pair).wait_recv()
        passing(pair).start()

    for c in range(count):
        m, i, size = chunks[c]
        loading(c).wait()
        swapping(c).wait()
        if c + DEPTH < count:
            swapping(c + DEPTH).start()
        step = 32 if size % 32 == 0 else 16

        def average(k, carry, m=m, i=i, size=size, step=step):
            at = pl.ds(pl.multiple_of(i * size + k * step, step), step)
            mine = held[m][at].astype(jnp.float32)
            other = landed[m][at].astype(jnp.float32)
            landed[m][at] = ((mine + other) * 0.5).astype(jnp.bfloat16)
            return carry

        lax.fori_loop(0, size // step, average, 0)
        storing(c).start()
        if not shared:
            fetching(c).start()
        elif c % 2 == 1:
            fetching_half(c // 2).start()
            if c >= 5:
                pass_on(passed)
                passed += 1
        if c == token_step:
            tokens_out.wait_recv()
            for copy in spread:
                copy.start()
    if shared:
        for pair in range(passed, count // 2):
            pass_on(pair)
        for pair in range(count // 2):
            fetching_half(pair).wait_send()
            passing(pair).wait()
    else:
        for c in range(count):
            fetching(c).wait()
    for c in range(count):
        storing(c).wait()
    tokens_out.wait_send()
    for copy in spread + early:
        copy.wait()


def stream(first, second, number, operands):
    weights, tokens, rate = operands
    ranks = lax.axis_size("tensor")
    count = sum(parts_of(w.shape[0]) for w in weights)
    like = [jax.ShapeDtypeStruct(w.shape, w.dtype) for w in weights]
    theirs = jax.ShapeDtypeStruct(
        tokens.shape[:-1] + (tokens.shape[-1] * ranks,), tokens.dtype
    )
    whole = pl.BlockSpec(memory_space=pl.ANY)
    held = [pltpu.VMEM(w.shape, w.dtype) for w in weights]
    size = sum(w.size * 2 for w in weights)
    result = pl.pallas_call(
        partial(kernel, first, second, ranks),
        out_shape=like + like + [theirs, theirs, jax.ShapeDtypeStruct(rate.shape, rate.dtype)],
        in_specs=[whole] * 5,
        out_specs=[whole] * 9,
        scratch_shapes=held
        + held
        + [pltpu.SemaphoreType.DMA((count,))] * 8
        + [pltpu.SemaphoreType.DMA((2 * ranks + 1,))] * 2,
        compiler_params=pltpu.CompilerParams(
            collective_id=number, has_side_effects=True, vmem_limit_bytes=48 * 2**20
        ),
        cost_estimate=pl.CostEstimate(flops=size, bytes_accessed=4 * size, transcendentals=0),
        name=f"stream_{first}_{second}",
    )(*weights, tokens, rate)
    return tuple(result[:3]), tuple(result[3:6]), result[6], result[7], result[8]


def local(inputs, out_grads, gate_weight, up_weight, down_weight, rates, partner_bits):
    weights = (gate_weight[0], up_weight[0], down_weight[0])
    rate = rates[0]
    x, dy = gather(inputs[0]), gather(out_grads[0])
    tokens = jnp.stack([inputs[1], out_grads[1]])

    hidden, d_gate, d_up = forward(weights, x, dy)
    scale = scale_of(rate, lax.psum(squares_of(x, dy, hidden, d_gate, d_up), "tensor"))
    results = [output(hidden, weights[2])]
    scale = scale[None]
    updated = (
        update(False, scale, (weights[0], x, d_gate)),
        update(False, scale, (weights[1], x, d_up)),
        update(True, scale, (weights[2], hidden.T, dy)),
    )

    bits = len(COST)
    plans = [(a, b) for a in range(bits) for b in range(bits) if a != b]
    first, second = partner_bits[0], partner_bits[1]
    index = first * (bits - 1) + second - (second > first).astype(second.dtype)
    own, far, theirs, mine, far_rate = lax.switch(
        index,
        [partial(stream, a, b, number) for number, (a, b) in enumerate(plans)],
        (updated, tokens, jnp.full((8, 128), rate)),
    )

    hidden, d_gate, d_up = forward(own, mine[0], mine[1])
    far_hidden, far_gate, far_up = forward(far, theirs[0], theirs[1])
    squares = lax.psum(
        jnp.stack(
            [
                squares_of(mine[0], mine[1], hidden, d_gate, d_up),
                squares_of(theirs[0], theirs[1], far_hidden, far_gate, far_up),
            ]
        ),
        "tensor",
    )
    results.append(output(hidden, own[2]))
    scale = jnp.stack([scale_of(rate, squares[0]), scale_of(far_rate[0, 0], squares[1])])
    done = (
        update(False, scale, (own[0], mine[0], d_gate), (far[0], theirs[0], far_gate)),
        update(False, scale, (own[1], mine[0], d_up), (far[1], theirs[0], far_up)),
        update(True, scale, (own[2], hidden.T, mine[1]), (far[2], far_hidden.T, theirs[1])),
    )
    return (done[0][None], done[1][None], done[2][None], jnp.stack(results))


def solution(mesh):
    return jax.shard_map(
        local,
        mesh=mesh,
        in_specs=(
            P(None, "replica", "tensor"),
            P(None, "replica", "tensor"),
            P("replica", None, "tensor"),
            P("replica", None, "tensor"),
            P("replica", "tensor", None),
            P("replica"),
            P(),
        ),
        out_specs=(
            P("replica", None, "tensor"),
            P("replica", None, "tensor"),
            P("replica", "tensor", None),
            P(None, "replica", "tensor"),
        ),
        check_vma=False,
    )
```
